256 devices in a mesh: row: 8 (over z_hi, core), col: 32 (over y, x, z_lo).
Axes of the slice: x: 4, y: 4, z: 8 (z_hi: 4, z_lo: 2; z = z_hi * 2 + z_lo), core: 2. Of those that a mesh axis runs over, the one named last changes fastest.
Arguments:
- tokens: bfloat16 [768, 8192], P('col', 'row'), may hold values from -6 to 6
- grad_out: bfloat16 [768, 8192], P('col', 'row'), may hold values from -6 to 6
- gate_weight: bfloat16 [8192, 28672], P('row', 'col'), may hold values from -0.0625 to 0.0625
- up_weight: bfloat16 [8192, 28672], P('row', 'col'), may hold values from -0.0625 to 0.0625
- down_weight: bfloat16 [28672, 8192], P('col', 'row'), may hold values from -0.03125 to 0.03125
Outputs:
- mixed: bfloat16 [768, 8192], P('col', 'row')
- grad_tokens: bfloat16 [768, 8192], P('col', 'row')
- grad_gate_weight: bfloat16 [8192, 28672], P('row', 'col')
- grad_up_weight: bfloat16 [8192, 28672], P('row', 'col')
- grad_down_weight: bfloat16 [28672, 8192], P('col', 'row')
The draws below stay inside these ranges and needn't reach their ends.
All inputs are finite; a program needn't handle non-finite values.
Results may differ from the reference program's by a relative error of at most 0.005.
Values may be sent and summed in bfloat16 or wider, within the bound.
No kernel may reach another device: no remote copies, remote signals or barrier semaphores. Data moves between devices by JAX's collectives and lax.ppermute only.
A program may use at most 128 MiB of HBM per device.

```python
import jax
import jax.numpy as jnp

D = 8192
FF = 28672
TOKENS = 768


def block_scale(rng, shape, cuts, smallest, largest):
    def one(axis_at, shards_of):
        draws = jax.random.uniform(jax.random.fold_in(jax.random.fold_in(rng, 6), axis_at), (shards_of,), jnp.float32, smallest / len(cuts), largest / len(cuts))
        return jnp.repeat(jnp.exp(draws), shape[axis_at] // shards_of).reshape((-1,) + (1,) * (len(shape) - axis_at - 1))

    gain = one(*cuts[0])
    for cut in cuts[1:]:
        gain = gain * one(*cut)
    return gain


def gaussian(stream_key, extent, scale, bound, split=(), held_as=jnp.bfloat16):
    array = jax.random.normal(stream_key, extent, jnp.float32) * scale
    if len(split) > 0:
        array = block_scale(stream_key, extent, split, -0.22, 0.18) * array
    return jnp.clip(array, min=-bound, max=bound).astype(held_as)


def setup_inputs(seed: int = 0) -> dict:
    arg_keys = jax.random.split(jax.random.key(seed), 6)
    return {
        "tokens": gaussian(arg_keys[0], (TOKENS, D), 1.0, 6.0, ((0, 32), (1, 8))),
        "grad_out": gaussian(arg_keys[1], (TOKENS, D), 1.0, 6.0, ((0, 32), (1, 8))),
        "gate_weight": gaussian(arg_keys[2], (D, FF), D ** -0.5, 0.0625, ((0, 8), (1, 32))),
        "up_weight": gaussian(arg_keys[3], (D, FF), D ** -0.5, 0.0625, ((0, 8), (1, 32))),
        "down_weight": gaussian(arg_keys[4], (FF, D), FF ** -0.5, 0.03125, ((0, 32), (1, 8))),
    }


def reference(tokens, grad_out, gate_weight, up_weight, down_weight):
    pre_gate = jnp.dot(tokens, gate_weight, preferred_element_type=jnp.float32)
    pre_up = jnp.dot(tokens, up_weight, preferred_element_type=jnp.float32)
    back_hidden = jnp.dot(grad_out, down_weight.T, preferred_element_type=jnp.float32)
    sigma = jax.nn.sigmoid(pre_gate)
    hidden = (pre_gate * sigma * pre_up).astype(jnp.bfloat16)
    grad_gate = (back_hidden * pre_up * sigma * (1.0 + pre_gate * (1.0 - sigma))).astype(jnp.bfloat16)
    grad_up = (back_hidden * pre_gate * sigma).astype(jnp.bfloat16)
    mixed = jnp.dot(hidden, down_weight, preferred_element_type=jnp.float32).astype(jnp.bfloat16)
    grad_tokens = (jnp.dot(grad_gate, gate_weight.T, preferred_element_type=jnp.float32)
                   + jnp.dot(grad_up, up_weight.T, preferred_element_type=jnp.float32)).astype(jnp.bfloat16)
    grad_gate_weight = jnp.dot(tokens.T, grad_gate, preferred_element_type=jnp.float32).astype(jnp.bfloat16)
    grad_up_weight = jnp.dot(tokens.T, grad_up, preferred_element_type=jnp.float32).astype(jnp.bfloat16)
    grad_down_weight = jnp.dot(hidden.T, grad_out, preferred_element_type=jnp.float32).astype(jnp.bfloat16)
    return (mixed, grad_tokens, grad_gate_weight, grad_up_weight, grad_down_weight)
```

```python
import jax
import jax.numpy as jnp
from jax import lax
from jax.sharding import PartitionSpec as P

BF16 = jnp.bfloat16
F32 = jnp.float32
STRIDE = {"zhi": ("row", 2, 4), "core": ("row", 1, 2), "y": ("col", 8, 4), "x": ("col", 2, 4), "zlo": ("col", 1, 2)}


def shift(value, name, step):
    axis, stride, size = STRIDE[name]
    total = 8 if axis == "row" else 32
    pairs = []
    for here in range(total):
        at = (here // stride) % size
        pairs.append((here, here + (((at + step) % size) - at) * stride))
    return lax.ppermute(value, axis, pairs)


def fan(value, name):
    return [value] + [shift(value, name, step) for step in (1, 2, 3)]


def fan_sum(pieces, name):
    total = pieces[0].astype(F32)
    got = [shift(pieces[step].astype(BF16), name, -step) for step in (1, 2, 3)]
    for value in got:
        total = total + value.astype(F32)
    return total


def dot(left, right, dims, out=F32):
    return lax.dot_general(left, right, (dims, ((), ())), preferred_element_type=F32).astype(out)


def body(tokens, grad_out, gate_weight, up_weight, down_weight):
    rows, feats = tokens.shape
    units = gate_weight.shape[1]
    row = lax.axis_index("row")
    zhi, core = row // 2, row % 2

    tok = jnp.concatenate([tokens, shift(tokens, "zlo", 1)], axis=0)
    grd = jnp.concatenate([grad_out, shift(grad_out, "zlo", 1)], axis=0)
    tok_x = jnp.concatenate(fan(tok, "x"), axis=0)
    grd_y = jnp.concatenate(fan(grd, "y"), axis=0)
    tok_all = jnp.concatenate(fan(tok_x, "y"), axis=0)
    grd_all = jnp.stack([g.reshape(4, 2 * rows, feats) for g in fan(grd_y, "x")], axis=1).reshape(32 * rows, feats)

    sums = [
        dot(tok_all, gate_weight, ((1,), (0,))),
        dot(tok_all, up_weight, ((1,), (0,))),
        dot(grd_all, down_weight, ((1,), (1,))),
    ]
    half, quarter = 16 * rows, 4 * rows
    mine = [lax.dynamic_slice_in_dim(s, core * half, half, 0) for s in sums]
    other = [lax.dynamic_slice_in_dim(s, (1 - core) * half, half, 0).astype(BF16) for s in sums]
    other = shift(jnp.stack(other), "core", 1)
    both = jnp.stack(mine) + other.astype(F32)
    pieces = [
        lax.dynamic_slice_in_dim(both, ((zhi + 4 - step) % 4) * quarter, quarter, 1) for step in range(4)
    ]
    pre_gate, pre_up, back = fan_sum(pieces, "zhi")
    sigma = jax.nn.sigmoid(pre_gate)
    hidden = (pre_gate * sigma * pre_up).astype(BF16)
    grad_gate = (back * pre_up * sigma * (1.0 + pre_gate * (1.0 - sigma))).astype(BF16)
    grad_up = (back * pre_gate * sigma).astype(BF16)

    block = jnp.stack([hidden, grad_gate, grad_up])
    full = jnp.zeros((3, half, units), BF16)
    for step, got in enumerate(fan(block, "zhi")):
        full = lax.dynamic_update_slice_in_dim(full, got, ((zhi + 4 - step) % 4) * quarter, 1)
    swap = shift(full, "core", 1)
    low = jnp.where(core == 0, full, swap)
    high = jnp.where(core == 0, swap, full)
    hidden_all, gate_all, up_all = jnp.concatenate([low, high], axis=1)

    mixed = dot(hidden_all, down_weight, ((1,), (0,)), BF16)
    back_tok = (
        dot(gate_all, gate_weight, ((1,), (1,))) + dot(up_all, up_weight, ((1,), (1,)))
    ).astype(BF16)
    mixed = mixed.reshape(4, 8 * rows, feats)
    back_tok = back_tok.reshape(4, 4, 2 * rows, feats)
    mixed = fan_sum([mixed[s] for s in range(4)], "y").reshape(4, 2 * rows, feats)
    back_tok = fan_sum([back_tok[:, s] for s in range(4)], "x")
    mixed = fan_sum([mixed[s] for s in range(4)], "x").reshape(2, rows, feats)
    back_tok = fan_sum([back_tok[s] for s in range(4)], "y").reshape(2, rows, feats)
    mixed = (mixed[0] + shift(mixed[1], "zlo", 1)).astype(BF16)
    grad_tokens = (back_tok[0] + shift(back_tok[1], "zlo", 1)).astype(BF16)

    grad_gate_weight = dot(tok_all, gate_all, ((0,), (0,)), BF16)
    grad_up_weight = dot(tok_all, up_all, ((0,), (0,)), BF16)
    grad_down_weight = dot(hidden_all, grd_all, ((0,), (0,)), BF16)
    return (mixed, grad_tokens, grad_gate_weight, grad_up_weight, grad_down_weight)


def solution(mesh):
    spec = (P("col", "row"), P("col", "row"), P("row", "col"), P("row", "col"), P("col", "row"))
    return jax.shard_map(body, mesh=mesh, in_specs=spec, out_specs=spec, check_vma=False)
```

```python
import jax
import jax.numpy as jnp
from jax import lax
from jax.sharding import PartitionSpec as P

BF16 = jnp.bfloat16
F32 = jnp.float32
AXES = {"zhi": ("row", 2, 4), "core": ("row", 1, 2), "y": ("col", 8, 4), "x": ("col", 2, 4), "zlo": ("col", 1, 2)}


def shift(value, name, step):
    axis, stride, size = AXES[name]
    pairs = []
    for here in range(8 if axis == "row" else 32):
        at = (here // stride) % size
        pairs.append((here, here + ((at + step) % size - at) * stride))
    return lax.ppermute(value, axis, pairs)


def fan(value, name):
    two = shift(value, name, 2)
    return [value, shift(value, name, 1), two, shift(value, name, 3)]


def fan_sum(pieces, name):
    got = [shift(pieces[step].astype(BF16), name, -step) for step in (2, 1, 3)]
    return pieces[0].astype(F32) + sum(value.astype(F32) for value in got)


def dot(left, right, dims, out=F32):
    return lax.dot_general(left, right, (dims, ((), ())), preferred_element_type=F32).astype(out)


def after(value, done):
    return lax.optimization_barrier((value, done))[0]


def body(tokens, grad_out, gate_weight, up_weight, down_weight):
    rows, feats = tokens.shape
    units = gate_weight.shape[1]
    row = lax.axis_index("row")
    zhi, core = row // 2, row % 2

    tok = jnp.concatenate([tokens, shift(tokens, "zlo", 1)], axis=0)
    grd = jnp.concatenate([grad_out, shift(grad_out, "zlo", 1)], axis=0)
    tok_x = jnp.concatenate(fan(tok, "x"), axis=0)
    grd_y = jnp.concatenate(fan(grd, "y"), axis=0)
    tok_all = jnp.concatenate(fan(tok_x, "y"), axis=0)
    grd_all = jnp.stack([g.reshape(4, 2 * rows, feats) for g in fan(grd_y, "x")], axis=1).reshape(32 * rows, feats)

    block = 4 * rows

    def half(value, which):
        blocks = value.reshape(4, 2, block, value.shape[1])
        return lax.dynamic_index_in_dim(blocks, which, 1, keepdims=False).reshape(4 * block, value.shape[1])

    operands = (
        (tok_all, gate_weight, ((1,), (0,))),
        (tok_all, up_weight, ((1,), (0,))),
        (grd_all, down_weight, ((1,), (1,))),
    )
    received = [shift(dot(half(left, 1 - core), right, dims), "core", 1) for left, right, dims in operands]
    both = [dot(half(left, core), right, dims) + got for (left, right, dims), got in zip(operands, received)]

    def pieces(step):
        at = (zhi + step) % 4
        return [lax.dynamic_slice_in_dim(value, at * block, block, 0) for value in both]

    def join(values):
        return jnp.concatenate(values, axis=1)

    cut = block // 2
    far = join([value.astype(BF16) for value in pieces(2)])
    from_below = shift(far[:cut], "zhi", 1).astype(F32)
    from_above = shift(far[cut:], "zhi", -1).astype(F32)
    up, down = join(pieces(1)), join(pieces(3))
    up = jnp.concatenate([up[:cut] + from_below, up[cut:]]).astype(BF16)
    down = jnp.concatenate([down[:cut], down[cut:] + from_above]).astype(BF16)
    totals = join(pieces(0)) + shift(up, "zhi", 1).astype(F32) + shift(down, "zhi", -1).astype(F32)

    pre_gate, pre_up, back = totals[:, :units], totals[:, units : 2 * units], totals[:, 2 * units :]
    sigma = jax.nn.sigmoid(pre_gate)
    hidden = (pre_gate * sigma * pre_up).astype(BF16)
    grad_gate = (back * pre_up * sigma * (1.0 + pre_gate * (1.0 - sigma))).astype(BF16)
    grad_up = (back * pre_gate * sigma).astype(BF16)
    mine = join([hidden, grad_gate, grad_up])

    below, above = shift(mine, "zhi", 1), shift(mine, "zhi", -1)
    far = jnp.concatenate([shift(below[:cut], "zhi", 1), shift(above[cut:], "zhi", -1)])
    full = jnp.zeros((4, 2) + mine.shape, BF16)
    for step, piece in ((0, mine), (3, below), (1, above), (2, far)):
        at = (zhi + step) % 4
        full = lax.dynamic_update_slice(full, piece[None, None], (at, core, 0, 0))
        full = lax.dynamic_update_slice(full, shift(piece, "core", 1)[None, None], (at, 1 - core, 0, 0))
    full = full.reshape(32 * rows, 3 * units)
    hidden_all, gate_all, up_all = full[:, :units], full[:, units : 2 * units], full[:, 2 * units :]

    mixed = dot(hidden_all, down_weight, ((1,), (0,)), BF16)
    back_tok = (
        dot(gate_all, gate_weight, ((1,), (1,))) + dot(up_all, up_weight, ((1,), (1,)))
    ).astype(BF16)
    tok_late, grd_late = after((tok_all, grd_all), back_tok)
    mixed = mixed.reshape(4, 8 * rows, feats)
    back_tok = back_tok.reshape(4, 4, 2 * rows, feats)
    mixed = fan_sum([mixed[s] for s in range(4)], "y").reshape(4, 2 * rows, feats)
    back_tok = fan_sum([back_tok[:, s] for s in range(4)], "x")
    mixed = fan_sum([mixed[s] for s in range(4)], "x").reshape(2, rows, feats)
    back_tok = fan_sum([back_tok[s] for s in range(4)], "y").reshape(2, rows, feats)
    mixed = (mixed[0] + shift(mixed[1], "zlo", 1)).astype(BF16)
    grad_tokens = (back_tok[0] + shift(back_tok[1], "zlo", 1)).astype(BF16)

    grad_gate_weight = dot(tok_late, gate_all, ((0,), (0,)), BF16)
    grad_up_weight = dot(tok_late, up_all, ((0,), (0,)), BF16)
    grad_down_weight = dot(hidden_all, grd_late, ((0,), (0,)), BF16)
    return (mixed, grad_tokens, grad_gate_weight, grad_up_weight, grad_down_weight)


def solution(mesh):
    spec = (P("col", "row"), P("col", "row"), P("row", "col"), P("row", "col"), P("col", "row"))
    return jax.shard_map(body, mesh=mesh, in_specs=spec, out_specs=spec, check_vma=False)
```

```python
import functools

import jax
import jax.numpy as jnp
from jax import lax
from jax.experimental import pallas as pl
from jax.experimental.pallas import tpu as pltpu
from jax.sharding import PartitionSpec as P

BF16 = jnp.bfloat16
F32 = jnp.float32
AXES = {"zhi": ("row", 2, 4), "core": ("row", 1, 2), "y": ("col", 8, 4), "x": ("col", 2, 4), "zlo": ("col", 1, 2)}


def shift(value, name, step):
    axis, stride, size = AXES[name]
    pairs = []
    for here in range(8 if axis == "row" else 32):
        at = (here // stride) % size
        pairs.append((here, here + ((at + step) % size - at) * stride))
    return lax.ppermute(value, axis, pairs)


def fan(value, name):
    two = shift(value, name, 2)
    return [value, shift(value, name, 1), two, shift(value, name, 3)]


def fan_sum(pieces, name):
    got = [shift(pieces[step].astype(BF16), name, -step) for step in (2, 1, 3)]
    return pieces[0].astype(F32) + sum(value.astype(F32) for value in got)


def ring_fan(value, name):
    own, below, far_low, far_high, above = ring_pieces(value, name)
    return [own, below, jnp.concatenate([far_low, far_high]), above]


def ring_pieces(value, name):
    cut = value.shape[0] // 2
    below, above = shift(value, name, 1), shift(value, name, 3)
    return [value, below, shift(below[:cut], name, 1), shift(above[cut:], name, 3), above]


def ring_sum_first(pieces, name):
    own, one, far, three = pieces
    cut = far.shape[0] // 2
    far = far.astype(BF16)
    got_down, got_up = shift(far[:cut], name, 3), shift(far[cut:], name, 1)
    one = jnp.concatenate([one[:cut] + got_down.astype(F32), one[cut:]]).astype(BF16)
    three = jnp.concatenate([three[:cut], three[cut:] + got_up.astype(F32)]).astype(BF16)
    return own, one, three


def ring_sum_second(own, one, three, name):
    return own + shift(one, name, 3).astype(F32) + shift(three, name, 1).astype(F32)


def dot(left, right, dims, out=F32):
    return lax.dot_general(left, right, (dims, ((), ())), preferred_element_type=F32).astype(out)


VMEM = pl.BlockSpec(memory_space=pltpu.VMEM)
SMEM = pl.BlockSpec(memory_space=pltpu.SMEM)


def tok_rows(refs, half):
    p0, p1, p2a, p2b, p3 = refs
    if half is None:
        return [p0[...], p1[...], p2a[...], p2b[...], p3[...]]
    rows = p2a.shape[0]
    part = pl.ds(pl.multiple_of(half * rows, rows), rows)
    return [p0[part], p1[part], jnp.where(half == 0, p2a[...], p2b[...]), p3[part]]


def grd_rows(refs, half):
    p0, p1, p2a, p2b, p3 = refs
    rows = p0.shape[0] // 4
    values = []
    for slot in range(4):
        at = pl.ds(slot * rows, rows)
        p2 = p2a if slot < 2 else p2b
        third = p2[pl.ds(slot % 2 * rows, rows)]
        if half is None:
            values += [p0[at], p1[at], third, p3[at]]
        else:
            values += [jnp.where(half == 0, p0[at], third), jnp.where(half == 0, p1[at], p3[at])]
    return values


def fill(scratch, values):
    at = 0
    for value in values:
        scratch[pl.ds(at, value.shape[0])] = value
        at += value.shape[0]


def half_dot_kernel(rows_of, dims, half_ref, *refs):
    pieces, weight, rest = refs[:5], refs[5], refs[6:]
    out, scratch = rest[-2:]
    fill(scratch, rows_of(pieces, half_ref[0]))
    total = lax.dot_general(scratch[...], weight[...], (dims, ((), ())), preferred_element_type=F32)
    out[...] = total if len(rest) == 2 else total + rest[0][...]


def half_dot(rows_of, half, pieces, weight, dims, add=()):
    count, feats = 2 * pieces[0].shape[0], pieces[0].shape[1]
    units = weight.shape[1 - dims[1][0]]
    return pl.pallas_call(
        functools.partial(half_dot_kernel, rows_of, dims),
        out_shape=jax.ShapeDtypeStruct((count, units), F32),
        in_specs=[SMEM] + [VMEM] * (6 + len(add)),
        out_specs=VMEM,
        scratch_shapes=[pltpu.VMEM((count, feats), BF16)],
        cost_estimate=pl.CostEstimate(flops=2 * count * feats * units, bytes_accessed=4 * count * units, transcendentals=0),
        compiler_params=pltpu.CompilerParams(vmem_limit_bytes=32 * 1024 * 1024),
    )(half[None].astype(jnp.int32), *pieces, weight, *add)


def weight_grad_kernel(rows_of, first, *refs):
    pieces, other, out, scratch = refs[:5], refs[5], refs[6], refs[7]
    fill(scratch, rows_of(pieces, None))
    left, right = (scratch, other) if first else (other, scratch)
    out[...] = lax.dot_general(
        left[...], right[...], (((0,), (0,)), ((), ())), preferred_element_type=F32
    ).astype(out.dtype)


def weight_grad(rows_of, pieces, other, first):
    count, feats = other.shape[0], pieces[0].shape[1]
    shape = (feats, other.shape[1]) if first else (other.shape[1], feats)
    return pl.pallas_call(
        functools.partial(weight_grad_kernel, rows_of, first),
        out_shape=jax.ShapeDtypeStruct(shape, BF16),
        in_specs=[VMEM] * 6,
        out_specs=VMEM,
        scratch_shapes=[pltpu.VMEM((count, feats), BF16)],
        cost_estimate=pl.CostEstimate(flops=1000000, bytes_accessed=100000, transcendentals=0),
        compiler_params=pltpu.CompilerParams(vmem_limit_bytes=32 * 1024 * 1024),
    )(*pieces, other)


def join(values):
    return jnp.concatenate(values, axis=1)


def hold(*values):
    return lax.optimization_barrier(values)


def body(tokens, grad_out, gate_weight, up_weight, down_weight):
    rows, feats = tokens.shape
    units = gate_weight.shape[1]
    row = lax.axis_index("row")
    zhi, core = row // 2, row % 2

    tok = jnp.concatenate([tokens, shift(tokens, "zlo", 1)], axis=0)
    grd = jnp.concatenate([grad_out, shift(grad_out, "zlo", 1)], axis=0)
    tok_x = jnp.concatenate(fan(tok, "x"), axis=0)
    grd_y = jnp.concatenate(fan(grd, "y"), axis=0)
    tok_pieces, grd_pieces = ring_pieces(tok_x, "y"), ring_pieces(grd_y, "x")

    block = 4 * rows
    cut = block // 2

    operands = (
        (tok_rows, tok_pieces, gate_weight, ((1,), (0,))),
        (tok_rows, tok_pieces, up_weight, ((1,), (0,))),
        (grd_rows, grd_pieces, down_weight, ((1,), (1,))),
    )
    received = [shift(half_dot(of, 1 - core, *rest), "core", 1) for of, *rest in operands]
    sums = [half_dot(of, core, *rest, (got,)) for (of, *rest), got in zip(operands, received)]
    sums = hold(*sums)

    def z_sum_first(lo):
        def piece(step):
            at = (zhi + step) % 4 * block + lo
            return join([lax.dynamic_slice_in_dim(value, at, cut, 0) for value in sums])

        return ring_sum_first([piece(0), piece(3), piece(2), piece(1)], "zhi")

    def activate(totals):
        count = totals.shape[1] // 3
        pre_gate, pre_up, back = totals[:, :count], totals[:, count : 2 * count], totals[:, 2 * count :]
        sigma = jax.nn.sigmoid(pre_gate)
        hidden = (pre_gate * sigma * pre_up).astype(BF16)
        grad_gate = (back * pre_up * sigma * (1.0 + pre_gate * (1.0 - sigma))).astype(BF16)
        grad_up = (back * pre_gate * sigma).astype(BF16)
        return join([hidden, grad_gate, grad_up])

    full = jnp.zeros((4, 2, block, 3 * units), BF16)
    mine = [activate(ring_sum_second(*first, "zhi")) for first in [z_sum_first(0), z_sum_first(cut)]]
    for at, value in enumerate(mine):
        own, below, far, above = ring_fan(value, "zhi")
        near = jnp.stack([own, above, below])
        near_other, far_other = shift(near, "core", 1), shift(far, "core", 1)
        for step, here, there in (
            (0, own, near_other[0]), (1, above, near_other[1]), (3, below, near_other[2]), (2, far, far_other)
        ):
            place = (zhi + step) % 4
            full = lax.dynamic_update_slice(full, here[None, None], (place, core, at * cut, 0))
            full = lax.dynamic_update_slice(full, there[None, None], (place, 1 - core, at * cut, 0))
    full = full.reshape(32 * rows, 3 * units)
    hidden_all, gate_all, up_all = full[:, :units], full[:, units : 2 * units], full[:, 2 * units :]

    mixed = dot(hidden_all, down_weight, ((1,), (0,)))
    back_tok = dot(gate_all, gate_weight, ((1,), (1,))) + dot(up_all, up_weight, ((1,), (1,)))
    mixed = mixed.reshape(4, 8 * rows, feats)
    back_tok = back_tok.reshape(4, 4, 2 * rows, feats)
    mixed = ring_sum_first([mixed[s] for s in range(4)], "y")
    back_tok = ring_sum_first([back_tok[:, s] for s in range(4)], "x")
    mixed, back_tok, tok_pieces, grd_pieces = hold(mixed, back_tok, tok_pieces, grd_pieces)

    grad_gate_weight = weight_grad(tok_rows, tok_pieces, gate_all, True)
    grad_up_weight = weight_grad(tok_rows, tok_pieces, up_all, True)
    grad_down_weight = weight_grad(grd_rows, grd_pieces, hidden_all, False)

    mixed = ring_sum_second(*mixed, "y").reshape(4, 2 * rows, feats)
    back_tok = ring_sum_second(*back_tok, "x")
    mixed, back_tok, grad_gate_weight, grad_up_weight, grad_down_weight = hold(
        mixed, back_tok, grad_gate_weight, grad_up_weight, grad_down_weight
    )
    mixed = fan_sum([mixed[s] for s in range(4)], "x").reshape(2, rows, feats)
    back_tok = fan_sum([back_tok[s] for s in range(4)], "y").reshape(2, rows, feats)
    out = join([mixed[0], back_tok[0]]) + shift(join([mixed[1], back_tok[1]]), "zlo", 1)
    mixed, grad_tokens = out[:, :feats].astype(BF16), out[:, feats:].astype(BF16)
    return (mixed, grad_tokens, grad_gate_weight, grad_up_weight, grad_down_weight)


def solution(mesh):
    spec = (P("col", "row"), P("col", "row"), P("row", "col"), P("row", "col"), P("col", "row"))
    return jax.shard_map(body, mesh=mesh, in_specs=spec, out_specs=spec, check_vma=False)
```

```python
import functools

import jax
import jax.numpy as jnp
from jax import lax
from jax.experimental import pallas as pl
from jax.experimental.pallas import tpu as pltpu
from jax.sharding import PartitionSpec as P

BF16 = jnp.bfloat16
F32 = jnp.float32
AXES = {"zhi": ("row", 2, 4), "core": ("row", 1, 2), "y": ("col", 8, 4), "x": ("col", 2, 4), "zlo": ("col", 1, 2)}


def shift(value, name, step):
    axis, stride, size = AXES[name]
    pairs = []
    for here in range(8 if axis == "row" else 32):
        at = (here // stride) % size
        pairs.append((here, here + ((at + step) % size - at) * stride))
    return lax.ppermute(value, axis, pairs)


def fan(value, name):
    two = shift(value, name, 2)
    return [value, shift(value, name, 1), two, shift(value, name, 3)]


def fan_sum(pieces, name):
    got = [shift(pieces[step].astype(BF16), name, -step) for step in (2, 1, 3)]
    return pieces[0].astype(F32) + sum(value.astype(F32) for value in got)


def ring_fan(value, name):
    own, below, far_low, far_high, above = ring_pieces(value, name)
    return [own, below, jnp.concatenate([far_low, far_high]), above]


def ring_pieces(value, name):
    cut = value.shape[0] // 2
    below, above = shift(value, name, 1), shift(value, name, 3)
    return [value, below, shift(below[:cut], name, 1), shift(above[cut:], name, 3), above]


def ring_sum_first(pieces, name):
    own, one, far, three = pieces
    cut = far.shape[0] // 2
    far = far.astype(BF16)
    got_down, got_up = shift(far[:cut], name, 3), shift(far[cut:], name, 1)
    one = jnp.concatenate([one[:cut] + got_down.astype(F32), one[cut:]]).astype(BF16)
    three = jnp.concatenate([three[:cut], three[cut:] + got_up.astype(F32)]).astype(BF16)
    return own, one, three


def ring_sum_second(own, one, three, name):
    return own + shift(one, name, 3).astype(F32) + shift(three, name, 1).astype(F32)


def dot(left, right, dims, out=F32):
    return lax.dot_general(left, right, (dims, ((), ())), preferred_element_type=F32).astype(out)


VMEM = pl.BlockSpec(memory_space=pltpu.VMEM)
SMEM = pl.BlockSpec(memory_space=pltpu.SMEM)


def tok_moves(rows):
    moves = [(2, 0, 2 * rows, 0, rows), (3, 0, 2 * rows, 1, rows)]
    for slot, piece in ((0, 0), (1, 1), (3, 4)):
        moves += [(piece, half * rows, slot * rows, half, rows) for half in (0, 1)]
    return moves


def grd_moves(rows):
    rows //= 2
    moves = []
    for slot in range(4):
        third = (2, slot * rows) if slot < 2 else (3, (slot - 2) * rows)
        for at, (piece, row) in enumerate(((0, slot * rows), (1, slot * rows), third, (4, slot * rows))):
            moves.append((piece, row, (2 * slot + at % 2) * rows, at // 2, rows))
    return moves


def fill(scratch, pieces, moves, count):
    for piece, row, to, half, rows in moves:
        block = 4 * to // count
        at = block * count // 4 * 2 + half * count // 4 + to % (count // 4)
        scratch[pl.ds(at, rows)] = pieces[piece][pl.ds(row, rows)]


def sort_kernel(moves, count, core_ref, *refs):
    pieces, out, sems = refs[:5], refs[5], refs[6]
    copies = []
    for at, (piece, row, to, half, rows) in enumerate(moves):
        to = pl.multiple_of(jnp.where(core_ref[0] == half, count, 0) + to, rows)
        copies.append(pltpu.make_async_copy(pieces[piece].at[pl.ds(row, rows)], out.at[pl.ds(to, rows)], sems.at[at]))
    for copy in copies:
        copy.start()
    for copy in copies:
        copy.wait()


def sort_rows(moves_of, core, pieces):
    count, feats = 2 * pieces[0].shape[0], pieces[0].shape[1]
    moves = moves_of(count // 4)
    return pl.pallas_call(
        functools.partial(sort_kernel, moves, count),
        out_shape=jax.ShapeDtypeStruct((2 * count, feats), BF16),
        in_specs=[SMEM] + [pl.BlockSpec(memory_space=pl.ANY)] * 5,
        out_specs=VMEM,
        scratch_shapes=[pltpu.SemaphoreType.DMA((len(moves),))],
        cost_estimate=pl.CostEstimate(flops=0, bytes_accessed=4 * count * feats, transcendentals=0),
        compiler_params=pltpu.CompilerParams(vmem_limit_bytes=32 * 1024 * 1024),
    )(core[None].astype(jnp.int32), *pieces)


def weight_grad_kernel(moves_of, first, *refs):
    pieces, other, out, scratch = refs[:5], refs[5], refs[6], refs[7]
    count = scratch.shape[0] // 2
    fill(scratch, pieces, moves_of(count // 4), count)
    left, right = (scratch, other) if first else (other, scratch)
    out[...] = lax.dot_general(
        left[...], right[...], (((0,), (0,)), ((), ())), preferred_element_type=F32
    ).astype(out.dtype)


def weight_grad(moves_of, pieces, other, first):
    count, feats = other.shape[0], pieces[0].shape[1]
    shape = (feats, other.shape[1]) if first else (other.shape[1], feats)
    return pl.pallas_call(
        functools.partial(weight_grad_kernel, moves_of, first),
        out_shape=jax.ShapeDtypeStruct(shape, BF16),
        in_specs=[VMEM] * 6,
        out_specs=VMEM,
        scratch_shapes=[pltpu.VMEM((count, feats), BF16)],
        cost_estimate=pl.CostEstimate(flops=1000000, bytes_accessed=100000, transcendentals=0),
        compiler_params=pltpu.CompilerParams(vmem_limit_bytes=32 * 1024 * 1024),
    )(*pieces, other)


def join(values):
    return jnp.concatenate(values, axis=1)


def hold(*values):
    return lax.optimization_barrier(values)


def body(tokens, grad_out, gate_weight, up_weight, down_weight):
    rows, feats = tokens.shape
    units = gate_weight.shape[1]
    row = lax.axis_index("row")
    zhi, core = row // 2, row % 2

    tok = jnp.concatenate([tokens, shift(tokens, "zlo", 1)], axis=0)
    grd = jnp.concatenate([grad_out, shift(grad_out, "zlo", 1)], axis=0)
    tok_x = jnp.concatenate(fan(tok, "x"), axis=0)
    grd_y = jnp.concatenate(fan(grd, "y"), axis=0)
    tok_pieces, grd_pieces = ring_pieces(tok_x, "y"), ring_pieces(grd_y, "x")

    block = 4 * rows
    cut = block // 2

    tok_sorted = sort_rows(tok_moves, core, tok_pieces)
    grd_sorted = sort_rows(grd_moves, core, grd_pieces)
    sums = [
        dot(tok_sorted, gate_weight, ((1,), (0,))),
        dot(tok_sorted, up_weight, ((1,), (0,))),
        dot(grd_sorted, down_weight, ((1,), (1,))),
    ]
    sums = [value[4 * block :] + shift(value[: 4 * block], "core", 1) for value in sums]
    sums = hold(*sums)

    def z_sum_first(lo):
        def piece(step):
            at = (zhi + step) % 4 * block + lo
            return join([lax.dynamic_slice_in_dim(value, at, cut, 0) for value in sums])

        return ring_sum_first([piece(0), piece(3), piece(2), piece(1)], "zhi")

    def activate(totals):
        count = totals.shape[1] // 3
        pre_gate, pre_up, back = totals[:, :count], totals[:, count : 2 * count], totals[:, 2 * count :]
        sigma = jax.nn.sigmoid(pre_gate)
        hidden = (pre_gate * sigma * pre_up).astype(BF16)
        grad_gate = (back * pre_up * sigma * (1.0 + pre_gate * (1.0 - sigma))).astype(BF16)
        grad_up = (back * pre_gate * sigma).astype(BF16)
        return join([hidden, grad_gate, grad_up])

    full = jnp.zeros((4, 2, block, 3 * units), BF16)
    mine = [activate(ring_sum_second(*first, "zhi")) for first in [z_sum_first(0), z_sum_first(cut)]]
    for at, value in enumerate(mine):
        own, below, far, above = ring_fan(value, "zhi")
        near = jnp.stack([own, above, below])
        near_other, far_other = shift(near, "core", 1), shift(far, "core", 1)
        for step, here, there in (
            (0, own, near_other[0]), (1, above, near_other[1]), (3, below, near_other[2]), (2, far, far_other)
        ):
            place = (zhi + step) % 4
            full = lax.dynamic_update_slice(full, here[None, None], (place, core, at * cut, 0))
            full = lax.dynamic_update_slice(full, there[None, None], (place, 1 - core, at * cut, 0))
    full = full.reshape(32 * rows, 3 * units)
    hidden_all, gate_all, up_all = full[:, :units], full[:, units : 2 * units], full[:, 2 * units :]

    mixed = dot(hidden_all, down_weight, ((1,), (0,)))
    back_tok = dot(gate_all, gate_weight, ((1,), (1,))) + dot(up_all, up_weight, ((1,), (1,)))
    mixed = mixed.reshape(4, 8 * rows, feats)
    back_tok = back_tok.reshape(4, 4, 2 * rows, feats)
    mixed = ring_sum_first([mixed[s] for s in range(4)], "y")
    back_tok = ring_sum_first([back_tok[:, s] for s in range(4)], "x")
    mixed, back_tok, tok_pieces, grd_pieces = hold(mixed, back_tok, tok_pieces, grd_pieces)

    grad_gate_weight = weight_grad(tok_moves, tok_pieces, gate_all, True)
    grad_up_weight = weight_grad(tok_moves, tok_pieces, up_all, True)

    mixed = ring_sum_second(*mixed, "y").reshape(4, 2 * rows, feats)
    back_tok = ring_sum_second(*back_tok, "x")
    mixed, back_tok, grad_gate_weight, grad_up_weight = hold(mixed, back_tok, grad_gate_weight, grad_up_weight)
    mixed = fan_sum([mixed[s] for s in range(4)], "x").reshape(2, rows, feats)
    back_tok = fan_sum([back_tok[s] for s in range(4)], "y").reshape(2, rows, feats)
    mixed, back_tok, grd_pieces = hold(mixed, back_tok, grd_pieces)
    grad_down_weight = weight_grad(grd_moves, grd_pieces, hidden_all, False)
    out = join([mixed[0], back_tok[0]]) + shift(join([mixed[1], back_tok[1]]), "zlo", 1)
    mixed, grad_tokens = out[:, :feats].astype(BF16), out[:, feats:].astype(BF16)
    return (mixed, grad_tokens, grad_gate_weight, grad_up_weight, grad_down_weight)


def solution(mesh):
    spec = (P("col", "row"), P("col", "row"), P("row", "col"), P("row", "col"), P("col", "row"))
    return jax.shard_map(body, mesh=mesh, in_specs=spec, out_specs=spec, check_vma=False)
```

```python
import functools

import jax
import jax.numpy as jnp
from jax import lax
from jax.experimental import pallas as pl
from jax.experimental.pallas import tpu as pltpu
from jax.sharding import PartitionSpec as P

BF16 = jnp.bfloat16
F32 = jnp.float32
AXES = {"zhi": ("row", 2, 4), "core": ("row", 1, 2), "y": ("col", 8, 4), "x": ("col", 2, 4), "zlo": ("col", 1, 2)}


def shift(value, name, step):
    axis, stride, size = AXES[name]
    pairs = []
    for here in range(8 if axis == "row" else 32):
        at = (here // stride) % size
        pairs.append((here, here + ((at + step) % size - at) * stride))
    return lax.ppermute(value, axis, pairs)


def fan(value, name):
    two = shift(value, name, 2)
    return [value, shift(value, name, 1), two, shift(value, name, 3)]


def fan_sum(pieces, name):
    got = [shift(pieces[step].astype(BF16), name, -step) for step in (2, 1, 3)]
    return pieces[0].astype(F32) + sum(value.astype(F32) for value in got)


def ring_fan(value, name):
    own, below, far_low, far_high, above = ring_pieces(value, name)
    return [own, below, jnp.concatenate([far_low, far_high]), above]


def ring_pieces(value, name):
    cut = value.shape[0] // 2
    below, above = shift(value, name, 1), shift(value, name, 3)
    return [value, below, shift(below[:cut], name, 1), shift(above[cut:], name, 3), above]


def ring_sum_first(pieces, name):
    own, one, far, three = pieces
    cut = far.shape[0] // 2
    far = far.astype(BF16)
    got_down, got_up = shift(far[:cut], name, 3), shift(far[cut:], name, 1)
    one = jnp.concatenate([one[:cut] + got_down.astype(F32), one[cut:]]).astype(BF16)
    three = jnp.concatenate([three[:cut], three[cut:] + got_up.astype(F32)]).astype(BF16)
    return own, one, three


def ring_sum_second(own, one, three, name):
    return own + shift(one, name, 3).astype(F32) + shift(three, name, 1).astype(F32)


def dot(left, right, dims, out=F32):
    return lax.dot_general(left, right, (dims, ((), ())), preferred_element_type=F32).astype(out)


VMEM = pl.BlockSpec(memory_space=pltpu.VMEM)
SMEM = pl.BlockSpec(memory_space=pltpu.SMEM)


def tok_moves(rows):
    moves = [(2, 0, 2 * rows, 0, rows), (3, 0, 2 * rows, 1, rows)]
    for slot, piece in ((0, 0), (1, 1), (3, 4)):
        moves += [(piece, half * rows, slot * rows, half, rows) for half in (0, 1)]
    return moves


def grd_moves(rows):
    rows //= 2
    moves = []
    for slot in range(4):
        third = (2, slot * rows) if slot < 2 else (3, (slot - 2) * rows)
        for at, (piece, row) in enumerate(((0, slot * rows), (1, slot * rows), third, (4, slot * rows))):
            moves.append((piece, row, (2 * slot + at % 2) * rows, at // 2, rows))
    return moves


def fill(scratch, pieces, moves, count):
    for piece, row, to, half, rows in moves:
        block = 4 * to // count
        at = block * count // 4 * 2 + half * count // 4 + to % (count // 4)
        scratch[pl.ds(at, rows)] = pieces[piece][pl.ds(row, rows)]


def sort_kernel(moves, count, core_ref, *refs):
    pieces, out, sems = refs[:5], refs[5], refs[6]
    copies = []
    for at, (piece, row, to, half, rows) in enumerate(moves):
        to = pl.multiple_of(jnp.where(core_ref[0] == half, count, 0) + to, rows)
        copies.append(pltpu.make_async_copy(pieces[piece].at[pl.ds(row, rows)], out.at[pl.ds(to, rows)], sems.at[at]))
    for copy in copies:
        copy.start()
    for copy in copies:
        copy.wait()


def sort_rows(moves_of, core, pieces):
    count, feats = 2 * pieces[0].shape[0], pieces[0].shape[1]
    moves = moves_of(count // 4)
    return pl.pallas_call(
        functools.partial(sort_kernel, moves, count),
        out_shape=jax.ShapeDtypeStruct((2 * count, feats), BF16),
        in_specs=[SMEM] + [pl.BlockSpec(memory_space=pl.ANY)] * 5,
        out_specs=VMEM,
        scratch_shapes=[pltpu.SemaphoreType.DMA((len(moves),))],
        cost_estimate=pl.CostEstimate(flops=0, bytes_accessed=4 * count * feats, transcendentals=0),
        compiler_params=pltpu.CompilerParams(vmem_limit_bytes=32 * 1024 * 1024),
    )(core[None].astype(jnp.int32), *pieces)


def weight_grad_kernel(moves_of, first, *refs):
    pieces, other, out, scratch = refs[:5], refs[5], refs[6], refs[7]
    count = scratch.shape[0] // 2
    fill(scratch, pieces, moves_of(count // 4), count)
    left, right = (scratch, other) if first else (other, scratch)
    out[...] = lax.dot_general(
        left[...], right[...], (((0,), (0,)), ((), ())), preferred_element_type=F32
    ).astype(out.dtype)


def weight_grad(moves_of, pieces, other, first):
    count, feats = other.shape[0], pieces[0].shape[1]
    shape = (feats, other.shape[1]) if first else (other.shape[1], feats)
    return pl.pallas_call(
        functools.partial(weight_grad_kernel, moves_of, first),
        out_shape=jax.ShapeDtypeStruct(shape, BF16),
        in_specs=[VMEM] * 6,
        out_specs=VMEM,
        scratch_shapes=[pltpu.VMEM((count, feats), BF16)],
        cost_estimate=pl.CostEstimate(flops=1000000, bytes_accessed=100000, transcendentals=0),
        compiler_params=pltpu.CompilerParams(vmem_limit_bytes=32 * 1024 * 1024),
    )(*pieces, other)


def join(values):
    return jnp.concatenate(values, axis=1)


def hold(*values):
    return lax.optimization_barrier(values)


def body(tokens, grad_out, gate_weight, up_weight, down_weight):
    rows, feats = tokens.shape
    units = gate_weight.shape[1]
    row = lax.axis_index("row")
    zhi, core = row // 2, row % 2

    tok = jnp.concatenate([tokens, shift(tokens, "zlo", 1)], axis=0)
    grd = jnp.concatenate([grad_out, shift(grad_out, "zlo", 1)], axis=0)
    tok_x = jnp.concatenate(fan(tok, "x"), axis=0)
    grd_y = jnp.concatenate(fan(grd, "y"), axis=0)
    tok_pieces, grd_pieces = ring_pieces(tok_x, "y"), ring_pieces(grd_y, "x")

    block = 4 * rows
    cut = block // 2

    tok_sorted = sort_rows(tok_moves, core, tok_pieces)
    grd_sorted = sort_rows(grd_moves, core, grd_pieces)
    operands = (
        (tok_sorted, gate_weight, ((1,), (0,))),
        (tok_sorted, up_weight, ((1,), (0,))),
        (grd_sorted, down_weight, ((1,), (1,))),
    )
    received = [shift(dot(left[: 4 * block], right, dims), "core", 1) for left, right, dims in operands]
    sums = [dot(left[4 * block :], right, dims) + got for (left, right, dims), got in zip(operands, received)]
    sums = hold(*sums)

    def z_sum_first(lo):
        def piece(step):
            at = (zhi + step) % 4 * block + lo
            return join([lax.dynamic_slice_in_dim(value, at, cut, 0) for value in sums])

        return ring_sum_first([piece(0), piece(3), piece(2), piece(1)], "zhi")

    def activate(totals):
        count = totals.shape[1] // 3
        pre_gate, pre_up, back = totals[:, :count], totals[:, count : 2 * count], totals[:, 2 * count :]
        sigma = jax.nn.sigmoid(pre_gate)
        hidden = (pre_gate * sigma * pre_up).astype(BF16)
        grad_gate = (back * pre_up * sigma * (1.0 + pre_gate * (1.0 - sigma))).astype(BF16)
        grad_up = (back * pre_gate * sigma).astype(BF16)
        return join([hidden, grad_gate, grad_up])

    full = jnp.zeros((4, 2, block, 3 * units), BF16)
    mine = [activate(ring_sum_second(*first, "zhi")) for first in [z_sum_first(0), z_sum_first(cut)]]
    for at, value in enumerate(mine):
        own, below, far, above = ring_fan(value, "zhi")
        near = jnp.stack([own, above, below])
        near_other, far_other = shift(near, "core", 1), shift(far, "core", 1)
        for step, here, there in (
            (0, own, near_other[0]), (1, above, near_other[1]), (3, below, near_other[2]), (2, far, far_other)
        ):
            place = (zhi + step) % 4
            full = lax.dynamic_update_slice(full, here[None, None], (place, core, at * cut, 0))
            full = lax.dynamic_update_slice(full, there[None, None], (place, 1 - core, at * cut, 0))
    full = full.reshape(32 * rows, 3 * units)
    hidden_all, gate_all, up_all = full[:, :units], full[:, units : 2 * units], full[:, 2 * units :]

    mixed = dot(hidden_all, down_weight, ((1,), (0,)))
    back_tok = dot(gate_all, gate_weight, ((1,), (1,))) + dot(up_all, up_weight, ((1,), (1,)))
    mixed = mixed.reshape(4, 8 * rows, feats)
    back_tok = back_tok.reshape(4, 4, 2 * rows, feats)
    mixed = ring_sum_first([mixed[s] for s in range(4)], "y")
    back_tok = ring_sum_first([back_tok[:, s] for s in range(4)], "x")
    mixed, back_tok, tok_pieces, grd_pieces = hold(mixed, back_tok, tok_pieces, grd_pieces)

    grad_gate_weight = weight_grad(tok_moves, tok_pieces, gate_all, True)
    grad_up_weight = weight_grad(tok_moves, tok_pieces, up_all, True)

    mixed = ring_sum_second(*mixed, "y").reshape(4, 2 * rows, feats)
    back_tok = ring_sum_second(*back_tok, "x")
    mixed, back_tok, grad_gate_weight, grad_up_weight = hold(mixed, back_tok, grad_gate_weight, grad_up_weight)
    mixed = fan_sum([mixed[s] for s in range(4)], "x").reshape(2, rows, feats)
    back_tok = fan_sum([back_tok[s] for s in range(4)], "y").reshape(2, rows, feats)
    mixed, back_tok, grd_pieces = hold(mixed, back_tok, grd_pieces)
    grad_down_weight = weight_grad(grd_moves, grd_pieces, hidden_all, False)
    out = join([mixed[0], back_tok[0]]) + shift(join([mixed[1], back_tok[1]]), "zlo", 1)
    mixed, grad_tokens = out[:, :feats].astype(BF16), out[:, feats:].astype(BF16)
    return (mixed, grad_tokens, grad_gate_weight, grad_up_weight, grad_down_weight)


def solution(mesh):
    spec = (P("col", "row"), P("col", "row"), P("row", "col"), P("row", "col"), P("col", "row"))
    return jax.shard_map(body, mesh=mesh, in_specs=spec, out_specs=spec, check_vma=False)
```
